512 devices in a mesh: row: 16 (over z_lo, y), col: 32 (over x, z_hi, core).
Axes of the slice: x: 4, y: 4, z: 16 (z_hi: 4, z_lo: 4; z = z_hi * 4 + z_lo), core: 2. Of those that a mesh axis runs over, the one named last changes fastest.
Arguments:
- hidden: bfloat16 [1024, 24576], P('col', 'row'), may hold values from -0.75 to 0.75
- weight: bfloat16 [24576, 12288], P('row', 'col'), may hold values from -0.0390625 to 0.0390625
- out_grad: bfloat16 [1024, 12288], P('row', 'col'), may hold values from -1.5 to 1.5
Outputs:
- input_grad: bfloat16 [1024, 24576], P('col', 'row')
- weight_grad: bfloat16 [24576, 12288], P('row', 'col')
The draws below stay inside these ranges and needn't reach their ends.
All inputs are finite; a program needn't handle non-finite values.
Results may differ from the reference program's by a relative error of at most 0.019.
Values may be sent and summed in bfloat16 or wider, within the bound.
A program may use at most 64 MiB of HBM per device.

```python
import jax
import jax.numpy as jnp
from jax import lax

D = 12288
FF = 24576
TOKENS = 1024
N_COL = 32


def raised(values, stream_key, source, target, shards_of, factor):
    def block_of(dim):
        return (jnp.arange(values.shape[dim]) // (values.shape[dim] // shards_of)).reshape((-1,) + (1,) * (values.ndim - 1 - dim))

    one_side = jax.random.permutation(stream_key, shards_of)[block_of(target)]
    other_side = (block_of(target) + shards_of // 2) % shards_of
    return jnp.where((block_of(source) == one_side) | (block_of(source) == other_side), factor * values, values)


def level_of(own_key, shape, split, least, top_value):
    gain, own = 1.0, jax.random.fold_in(own_key, 6)
    for axis_at, shards_of in split:
        draws = jnp.exp(jax.random.uniform(jax.random.fold_in(own, axis_at), (shards_of,), jnp.float32, least / len(split), top_value / len(split)))
        gain = gain * jnp.repeat(draws, shape[axis_at] // shards_of).reshape([-1 if axis == axis_at else 1 for axis in range(len(shape))])
    return gain


def gaussian(own_key, shape, scale, bound, cuts=(), kind=jnp.bfloat16):
    array = scale * jax.random.normal(own_key, shape, jnp.float32)
    if cuts:
        array = array * level_of(own_key, shape, cuts, -0.22, 0.18)
    return jnp.clip(array, -bound, bound).astype(kind)


def bell_draw_with(stream_key, extent, scale, reach, pieces, heavy, kind=jnp.bfloat16):
    array = scale * jax.random.normal(stream_key, extent, jnp.float32)
    if pieces:
        array = array * level_of(stream_key, extent, pieces, -0.22, 0.18)
    return jnp.clip(raised(array, jax.random.fold_in(stream_key, 3), *heavy), -reach, reach).astype(kind)


def setup_inputs(seed: int = 0) -> dict:
    streams_of = jax.random.split(jax.random.key(seed), 4)
    return {
        "hidden": gaussian(streams_of[0], (TOKENS, FF), 0.125, 0.75, ((0, 32), (1, 16))),
        "weight": gaussian(streams_of[1], (FF, D), FF ** -0.5, 0.0390625, ((0, 16), (1, 32))),
        "out_grad": bell_draw_with(streams_of[2], (TOKENS, D), 0.25, 1.5, ((0, 16), (1, 32)), (1, 0, 32, 2.75)),
    }


def reference(hidden, weight, out_grad):
    width = D // N_COL

    def add_block(total, index):
        start = index * width
        grads = lax.dynamic_slice_in_dim(out_grad, start, width, 1)
        columns = lax.dynamic_slice_in_dim(weight, start, width, 1)
        term = lax.dot_general(grads, columns, (((1,), (1,)), ((), ())), preferred_element_type=jnp.float32)
        rounded = lax.optimization_barrier(term.astype(jnp.bfloat16))
        return total + rounded.astype(jnp.float32), None

    indices = jnp.arange(N_COL, dtype=jnp.int32)
    total, unused = lax.scan(add_block, jnp.zeros((TOKENS, FF), jnp.float32), indices)
    input_grad = total.astype(jnp.bfloat16)
    weight_grad = jnp.dot(hidden.T, out_grad, preferred_element_type=jnp.float32).astype(jnp.bfloat16)
    return input_grad, weight_grad
```

```python
import jax
import jax.numpy as jnp
from jax import lax
from jax.experimental import pallas as pl
from jax.experimental.pallas import tpu as pltpu
from jax.sharding import PartitionSpec as P

BF16, F32 = jnp.bfloat16, jnp.float32
FF, D, T = 1536, 384, 32
A, B = pl.ds(0, T // 2), pl.ds(T // 2, T // 2)
SENDS = 96


def kernel(
    h_ref, w_ref, g_ref, ig_ref, wg_ref,
    hall, gall, gsib, wall, part, ra, rb, r2p, r2m, summed, za, zb, z2p, z2m, acc,
    send_sem, recv_sem, local_sem,
):
    r, c = lax.axis_index("row"), lax.axis_index("col")
    zl, y = r // 4, r % 4
    x, zh, k = c // 8, (c // 2) % 4, c % 2

    def at(dzl=0, dy=0, dx=0, dzh=0, dk=0):
        row = ((zl + dzl) % 4) * 4 + (y + dy) % 4
        col = (((x + dx) % 4) * 4 + (zh + dzh) % 4) * 2 + (k + dk) % 2
        return (row, col)

    started = []

    def send(src, dst, to):
        i = len(started)
        copy = pltpu.make_async_remote_copy(
            src_ref=src, dst_ref=dst, send_sem=send_sem.at[i], recv_sem=recv_sem.at[i],
            device_id=to, device_id_type=pl.DeviceIdType.MESH,
        )
        copy.start()
        started.append(copy)
        return copy

    load_w = pltpu.make_async_copy(w_ref, wall.at[:, pl.ds(0, D)], local_sem.at[0])
    load_g = pltpu.make_async_copy(g_ref, gall.at[y, zl], local_sem.at[1])
    load_h = pltpu.make_async_copy(h_ref, hall.at[zh, x, k], local_sem.at[2])
    for load in (load_g, load_h, load_w):
        load.start()

    partners = [at(dzl=1), at(dzl=2), at(dzl=3), at(dy=1), at(dy=2), at(dy=3)]
    partners += [at(dx=1), at(dx=3), at(dzh=1), at(dzh=3), at(dk=1)]
    barrier = pltpu.get_barrier_semaphore()
    for partner in partners:
        pl.semaphore_signal(barrier, inc=1, device_id=partner, device_id_type=pl.DeviceIdType.MESH)
    pl.semaphore_wait(barrier, len(partners))

    right, left, up, down, sib = at(dx=1), at(dx=3), at(dzh=1), at(dzh=3), at(dk=1)
    xr, xl, x2 = (x + 1) % 4, (x + 3) % 4, (x + 2) % 4
    zu, zd, z2 = (zh + 1) % 4, (zh + 3) % 4, (zh + 2) % 4

    g_zl = {d: send(g_ref, gall.at[y, zl], at(dzl=d)) for d in (1, 3, 2)}
    g_y = {(0, d): send(g_ref, gall.at[y, zl], at(dy=d)) for d in (1, 3, 2)}
    w_sib = send(w_ref, wall.at[:, pl.ds(D, D)], sib)
    hz_a = send(h_ref.at[A], hall.at[zh, x, k, A], up)
    hz_b = send(h_ref.at[B], hall.at[zh, x, k, B], down)
    hx = {}
    load_h.wait()

    def h_x_half(q, zq, half):
        block = hall.at[zq, x, k, half]
        hx[q, "a" if half is A else "b", "r"] = send(block, block, right)
        hx[q, "a" if half is A else "b", "l"] = send(block, block, left)

    def h_x_forward(q, zq):
        hx[q, "a", "r"].wait_recv()
        block = hall.at[zq, xl, k, A]
        hx[q, "fa"] = send(block, block, right)
        hx[q, "b", "l"].wait_recv()
        block = hall.at[zq, xr, k, B]
        hx[q, "fb"] = send(block, block, left)

    def h_x_end(q, zq):
        for name in ((q, "b", "r"), (q, "a", "l"), (q, "fa"), (q, "fb")):
            hx[name].wait_recv()
        block = hall.at[zq, :, k]
        hx[q, "sib"] = send(block, block, sib)

    h_x_half(0, zh, A)
    h_x_half(0, zh, B)
    hz_a2 = send(h_ref.at[B], hall.at[zh, x, k, B], up)
    hz_b2 = send(h_ref.at[A], hall.at[zh, x, k, A], down)

    for d in (1, 3, 2):
        g_zl[d].wait_recv()
        block = gall.at[y, (zl - d + 4) % 4]
        for dy in (1, 3, 2):
            g_y[d, dy] = send(block, block, at(dy=dy))
    load_g.wait()

    def g_to_sib(b):
        return send(gall.at[b, :, 1 - k], gsib.at[b], sib)

    g_sib = [g_to_sib(y)]
    h_x_forward(0, zh)
    load_w.wait()
    w_sib.wait_recv()

    bs = [y, (y + 3) % 4, (y + 1) % 4, (y + 2) % 4]
    rs = {}

    def reduce_x_start(j):
        b = bs[j]
        g_sib[j].wait_recv()
        grads = jnp.concatenate([gall[b, :, k].reshape(4 * T, D), gsib[b].reshape(4 * T, D)], axis=1)
        for n in range(0, FF, 512):
            cols = pl.ds(n, 512)
            block = lax.dot_general(grads, wall[cols], (((1,), (1,)), ((), ())), preferred_element_type=F32)
            part[j, :, :, cols] = block.astype(BF16).reshape(4, T, 512)
        rs[j, "1a"] = send(part.at[j, x2, A], ra.at[j], right)
        rs[j, "1b"] = send(part.at[j, x2, B], rb.at[j], left)
        rs[j, "2a"] = send(part.at[j, xr, B], r2p.at[j, B], right)
        rs[j, "2b"] = send(part.at[j, xl, A], r2m.at[j, A], left)

    def reduce_x_forward(j):
        rs[j, "1a"].wait_recv()
        part[j, xr, A] = (part[j, xr, A].astype(F32) + ra[j].astype(F32)).astype(BF16)
        rs[j, "2c"] = send(part.at[j, xr, A], r2p.at[j, A], right)
        rs[j, "1b"].wait_recv()
        part[j, xl, B] = (part[j, xl, B].astype(F32) + rb[j].astype(F32)).astype(BF16)
        rs[j, "2d"] = send(part.at[j, xl, B], r2m.at[j, B], left)

    def reduce_x_end(j):
        for name in ("2a", "2b", "2c", "2d"):
            rs[j, name].wait_recv()
        summed[bs[j]] = (part[j, x].astype(F32) + r2p[j].astype(F32) + r2m[j].astype(F32)).astype(BF16)

    reduce_x_start(0)
    hz_a.wait_recv()
    hz_fa = send(hall.at[zd, x, k, A], hall.at[zd, x, k, A], up)
    hz_b.wait_recv()
    hz_fb = send(hall.at[zu, x, k, B], hall.at[zu, x, k, B], down)
    for j, d in ((1, 1), (2, 3), (3, 2)):
        for e in (0, 1, 3, 2):
            g_y[e, d].wait_recv()
        g_sib.append(g_to_sib(bs[j]))
        reduce_x_forward(j - 1)
        reduce_x_start(j)
    h_x_end(0, zh)
    reduce_x_forward(3)

    def weight_grad(q, zq):
        hx[q, "sib"].wait_recv()
        grads = gall[zq].reshape(8 * T, D)
        for m in range(0, FF, 512):
            rows = pl.ds(m, 512)
            block = lax.dot_general(
                hall[zq, :, :, :, rows].reshape(8 * T, 512), grads, (((0,), (0,)), ((), ())), preferred_element_type=F32
            )
            if q == 0:
                acc[rows] = block
            elif q < 3:
                acc[rows] += block
            else:
                wg_ref[rows] = (acc[rows] + block).astype(BF16)

    hz_b2.wait_recv()
    hz_a2.wait_recv()
    h_x_half(1, zd, A)
    h_x_half(1, zd, B)
    h_x_half(2, zu, A)
    h_x_half(2, zu, B)

    for j in range(4):
        reduce_x_end(j)
    z1a = send(summed.at[z2, A], za, up)
    z1b = send(summed.at[z2, B], zb, down)
    z2a = send(summed.at[zu, B], z2p.at[B], up)
    z2b = send(summed.at[zd, A], z2m.at[A], down)
    weight_grad(0, zh)
    hz_fa.wait_recv()
    h_x_half(3, z2, A)
    hz_fb.wait_recv()
    h_x_half(3, z2, B)
    h_x_forward(1, zd)
    h_x_forward(2, zu)

    z1a.wait_recv()
    summed[zu, A] = (summed[zu, A].astype(F32) + za[...].astype(F32)).astype(BF16)
    z2c = send(summed.at[zu, A], z2p.at[A], up)
    z1b.wait_recv()
    summed[zd, B] = (summed[zd, B].astype(F32) + zb[...].astype(F32)).astype(BF16)
    z2d = send(summed.at[zd, B], z2m.at[B], down)

    h_x_forward(3, z2)
    h_x_end(1, zd)
    h_x_end(2, zu)
    weight_grad(1, zd)
    weight_grad(2, zu)
    h_x_end(3, z2)
    weight_grad(3, z2)

    for copy in (z2a, z2b, z2c, z2d):
        copy.wait_recv()
    ig_ref[...] = (summed[zh].astype(F32) + z2p[...].astype(F32) + z2m[...].astype(F32)).astype(BF16)
    for copy in started:
        copy.wait_send()


def shards(hidden, weight, out_grad):
    vmem = lambda *shape, dtype=BF16: pltpu.VMEM(shape, dtype)
    return pl.pallas_call(
        kernel,
        name="mlp_backward",
        out_shape=(jax.ShapeDtypeStruct((T, FF), BF16), jax.ShapeDtypeStruct((FF, D), BF16)),
        in_specs=[pl.BlockSpec(memory_space=pl.ANY)] * 3,
        out_specs=[pl.BlockSpec(memory_space=pltpu.VMEM)] * 2,
        scratch_shapes=[
            vmem(4, 4, 2, T, FF),
            vmem(4, 4, 2, T, D),
            vmem(4, 4, T, D),
            vmem(FF, 2 * D),
            vmem(4, 4, T, FF),
            vmem(4, T // 2, FF), vmem(4, T // 2, FF),
            vmem(4, T, FF), vmem(4, T, FF),
            vmem(4, T, FF),
            vmem(T // 2, FF), vmem(T // 2, FF),
            vmem(T, FF), vmem(T, FF),
            vmem(FF, D, dtype=F32),
            pltpu.SemaphoreType.DMA((SENDS,)),
            pltpu.SemaphoreType.DMA((SENDS,)),
            pltpu.SemaphoreType.DMA((3,)),
        ],
        compiler_params=pltpu.CompilerParams(
            collective_id=0, has_side_effects=True, vmem_limit_bytes=48 << 20
        ),
        cost_estimate=pl.CostEstimate(flops=2416 << 20, bytes_accessed=4 << 20, transcendentals=0),
    )(hidden, weight, out_grad.reshape(2, T, D))


def solution(mesh):
    in_specs = (P("col", "row"), P("row", "col"), P("row", "col"))
    out_specs = (P("col", "row"), P("row", "col"))
    return jax.shard_map(shards, mesh=mesh, in_specs=in_specs, out_specs=out_specs, check_vma=False)
```

```python
import jax
import jax.numpy as jnp
from jax import lax
from jax.experimental import pallas as pl
from jax.experimental.pallas import tpu as pltpu
from jax.sharding import PartitionSpec as P

BF16, F32 = jnp.bfloat16, jnp.float32
FF, D, T = 1536, 384, 32
A, B = pl.ds(0, T // 2), pl.ds(T // 2, T // 2)
SENDS = 84
ORDER = [('hx', 0, 'a'), ('hx', 0, 'b'), ('gy', 1), ('gy', 3), ('gy', 2), ('gs', 0), ('hxf', 0, 'a'), ('hxf', 0, 'b'), ('p', 0), ('rx', 0), ('hz1',), ('gs', 1), ('gs', 3), ('gs', 2), ('rf', 0), ('p', 1), ('rx', 1), ('hzf',), ('hz2',), ('hx', 1, 'a'), ('hx', 2, 'b'), ('p', 2), ('rx', 2), ('re', 0), ('rf', 1), ('hxf', 1, 'a'), ('hxf', 2, 'b'), ('p', 3), ('rx', 3), ('re', 1), ('rz', '1'), ('rf', 2), ('hs', 0), ('hx', 1, 'b'), ('hx', 2, 'a'), ('re', 2), ('rz', '2b'), ('rf', 3), ('hx', 3, 'a'), ('hx', 3, 'b'), ('hxf', 1, 'b'), ('hxf', 2, 'a'), ('re', 3), ('rz', '2a'), ('hs', 1), ('hs', 2), ('wg', 0), ('rz', '2c'), ('rz', '2d'), ('hxf', 3, 'a'), ('hxf', 3, 'b'), ('wg', 1), ('wg', 2), ('hs', 3), ('wg', 3)]


def kernel(
    h_ref, w_ref, g_ref, ig_ref, wg_ref,
    hall, gall, gsib, wall, part, ra, rb, r2p, r2m, summed, za, zb, z2p, z2m, acc,
    send_sem, recv_sem, local_sem, near_sem, far_sem,
):
    r, c = lax.axis_index("row"), lax.axis_index("col")
    zl, y = r // 4, r % 4
    x, zh, k = c // 8, (c // 2) % 4, c % 2

    def at(dzl=0, dy=0, dx=0, dzh=0, dk=0):
        row = ((zl + dzl) % 4) * 4 + (y + dy) % 4
        col = (((x + dx) % 4) * 4 + (zh + dzh) % 4) * 2 + (k + dk) % 2
        return (row, col)

    started = []

    def send(src, dst, to):
        i = len(started)
        copy = pltpu.make_async_remote_copy(
            src_ref=src, dst_ref=dst, send_sem=send_sem.at[i], recv_sem=recv_sem.at[i],
            device_id=to, device_id_type=pl.DeviceIdType.MESH,
        )
        copy.start()
        started.append(copy)
        return copy

    load_w = pltpu.make_async_copy(w_ref, wall.at[:, pl.ds(0, D)], local_sem.at[0])
    load_g = pltpu.make_async_copy(g_ref, gall.at[y, zl], local_sem.at[1])
    load_h = pltpu.make_async_copy(h_ref, hall.at[zh, x, k], local_sem.at[2])
    for load in (load_g, load_h, load_w):
        load.start()

    barrier = pltpu.get_barrier_semaphore()

    def signal(semaphore, to):
        pl.semaphore_signal(semaphore, inc=1, device_id=to, device_id_type=pl.DeviceIdType.MESH)

    near = [dict(dzl=1), dict(dzl=2), dict(dzl=3), dict(dy=1), dict(dy=2), dict(dy=3), dict(dx=1), dict(dx=3)]
    for chip in near:
        signal(barrier, at(dk=1 - k, **chip))
    for chip in (dict(dzh=1), dict(dzh=3)):
        signal(barrier, at(dk=k, **chip))

    @pl.when(k == 0)
    def _():
        signal(barrier, at(dk=1))

    @pl.when(k == 1)
    def _():
        pl.semaphore_wait(barrier, 2 * len(near) + 1)
        signal(near_sem, at(dk=1))

    @pl.when(k == 0)
    def _():
        pl.semaphore_wait(near_sem, 1)

    right, left, up, down, sib = at(dx=1), at(dx=3), at(dzh=1), at(dzh=3), at(dk=1)
    xr, xl, x2 = (x + 1) % 4, (x + 3) % 4, (x + 2) % 4
    zu, zd, z2 = (zh + 1) % 4, (zh + 3) % 4, (zh + 2) % 4

    g_zl = {d: send(g_ref, gall.at[y, zl], at(dzl=d)) for d in (1, 3, 2)}
    g_y = {(0, d): send(g_ref, gall.at[y, zl], at(dy=d)) for d in (1, 3, 2)}
    w_sib = send(w_ref, wall.at[:, pl.ds(D, D)], sib)
    hx, rs, g_sib, hz, rz = {}, {}, {}, {}, {}
    load_h.wait()

    far = [z2, zd, zu, zh]
    at_y = jnp.where(y == z2, 0, jnp.where(y == zd, 1, jnp.where(y == zu, 2, 3)))
    bs = [y] + [jnp.where(i < at_y, far[i], far[i + 1]) for i in range(3)]
    zq = [zh, zd, zu, z2]

    def g_along_y(d):
        g_zl[d].wait_recv()
        block = gall.at[y, (zl - d + 4) % 4]
        for dy in (1, 3, 2):
            g_y[d, dy] = send(block, block, at(dy=dy))

    def g_to_sib(d):
        if d == 0:
            load_g.wait()
        else:
            for e in (0, 1, 3, 2):
                g_y[e, d].wait_recv()
        b = (y - d + 4) % 4
        g_sib[d] = send(gall.at[b, :, 1 - k], gsib.at[b], sib)

    def h_z_first():
        @pl.when(k == 0)
        def _():
            pl.semaphore_wait(barrier, 4)
            signal(far_sem, at(dk=1))

        @pl.when(k == 1)
        def _():
            pl.semaphore_wait(far_sem, 1)

        hz["1u"] = send(h_ref.at[A], hall.at[zh, x, k, A], up)
        hz["1d"] = send(h_ref.at[B], hall.at[zh, x, k, B], down)

    def h_z_second():
        hz["2u"] = send(h_ref.at[B], hall.at[zh, x, k, B], up)
        hz["2d"] = send(h_ref.at[A], hall.at[zh, x, k, A], down)

    def h_z_forward():
        hz["1u"].wait_recv()
        hz["fa"] = send(hall.at[zd, x, k, A], hall.at[zd, x, k, A], up)
        hz["1d"].wait_recv()
        hz["fb"] = send(hall.at[zu, x, k, B], hall.at[zu, x, k, B], down)

    def h_x(q, name):
        after = {(1, "b"): "2u", (2, "a"): "2d", (3, "a"): "fa", (3, "b"): "fb"}.get((q, name))
        if after:
            hz[after].wait_recv()
        block = hall.at[zq[q], x, k, A if name == "a" else B]
        hx[q, name, "r"] = send(block, block, right)
        hx[q, name, "l"] = send(block, block, left)

    def h_x_forward(q, name):
        hx[q, name, "r" if name == "a" else "l"].wait_recv()
        block = hall.at[zq[q], xl, k, A] if name == "a" else hall.at[zq[q], xr, k, B]
        hx[q, "f" + name] = send(block, block, right if name == "a" else left)

    def h_to_sib(q):
        for name in ((q, "b", "r"), (q, "a", "l"), (q, "fa"), (q, "fb")):
            hx[name].wait_recv()
        block = hall.at[zq[q], :, k]
        hx[q, "sib"] = send(block, block, sib)

    def product(j):
        if j == 0:
            load_w.wait()
            w_sib.wait_recv()
            g_sib[0].wait_recv()
        if j == 1:
            for d in (1, 3, 2):
                g_sib[d].wait_recv()
        b = bs[j]
        grads = jnp.concatenate([gall[b, :, k].reshape(4 * T, D), gsib[b].reshape(4 * T, D)], axis=1)
        for n in range(0, FF, 512):
            cols = pl.ds(n, 512)
            block = lax.dot_general(grads, wall[cols], (((1,), (1,)), ((), ())), preferred_element_type=F32)
            part[j, :, :, cols] = block.astype(BF16).reshape(4, T, 512)

    def reduce_x(j):
        rs[j, "1a"] = send(part.at[j, x2, A], ra.at[j], right)
        rs[j, "1b"] = send(part.at[j, x2, B], rb.at[j], left)
        rs[j, "2a"] = send(part.at[j, xr, B], r2p.at[j, B], right)
        rs[j, "2b"] = send(part.at[j, xl, A], r2m.at[j, A], left)

    def reduce_x_forward(j):
        rs[j, "1a"].wait_recv()
        part[j, xr, A] = (part[j, xr, A].astype(F32) + ra[j].astype(F32)).astype(BF16)
        rs[j, "2c"] = send(part.at[j, xr, A], r2p.at[j, A], right)
        rs[j, "1b"].wait_recv()
        part[j, xl, B] = (part[j, xl, B].astype(F32) + rb[j].astype(F32)).astype(BF16)
        rs[j, "2d"] = send(part.at[j, xl, B], r2m.at[j, B], left)

    def reduce_x_end(j):
        for name in ("2a", "2b", "2c", "2d"):
            rs[j, name].wait_recv()
        summed[bs[j]] = (part[j, x].astype(F32) + r2p[j].astype(F32) + r2m[j].astype(F32)).astype(BF16)

    def reduce_z(name):
        if name == "1":
            rz["1a"] = send(summed.at[z2, A], za, up)
            rz["1b"] = send(summed.at[z2, B], zb, down)
        elif name == "2a":
            rz["2a"] = send(summed.at[zu, B], z2p.at[B], up)
        elif name == "2b":
            rz["2b"] = send(summed.at[zd, A], z2m.at[A], down)
        elif name == "2c":
            rz["1a"].wait_recv()
            summed[zu, A] = (summed[zu, A].astype(F32) + za[...].astype(F32)).astype(BF16)
            rz["2c"] = send(summed.at[zu, A], z2p.at[A], up)
        elif name == "2d":
            rz["1b"].wait_recv()
            summed[zd, B] = (summed[zd, B].astype(F32) + zb[...].astype(F32)).astype(BF16)
            rz["2d"] = send(summed.at[zd, B], z2m.at[B], down)

    def weight_grad(q):
        hx[q, "sib"].wait_recv()
        grads = gall[zq[q]].reshape(8 * T, D)
        for m in range(0, FF, 512):
            rows = pl.ds(m, 512)
            block = lax.dot_general(
                hall[zq[q], :, :, :, rows].reshape(8 * T, 512), grads, (((0,), (0,)), ((), ())),
                preferred_element_type=F32,
            )
            if q == 0:
                acc[rows] = block
            elif q < 3:
                acc[rows] += block
            else:
                wg_ref[rows] = (acc[rows] + block).astype(BF16)

    steps = {
        "gy": g_along_y, "gs": g_to_sib, "hz1": h_z_first, "hz2": h_z_second, "hzf": h_z_forward, "hx": h_x, "hxf": h_x_forward, "hs": h_to_sib,
        "p": product, "rx": reduce_x, "rf": reduce_x_forward, "re": reduce_x_end, "rz": reduce_z, "wg": weight_grad,
    }
    for step, *args in ORDER:
        steps[step](*args)

    for copy in (rz["2a"], rz["2b"], rz["2c"], rz["2d"]):
        copy.wait_recv()
    ig_ref[...] = (summed[zh].astype(F32) + z2p[...].astype(F32) + z2m[...].astype(F32)).astype(BF16)
    for copy in started:
        copy.wait_send()


def shards(hidden, weight, out_grad):
    vmem = lambda *shape, dtype=BF16: pltpu.VMEM(shape, dtype)
    return pl.pallas_call(
        kernel,
        name="mlp_backward",
        out_shape=(jax.ShapeDtypeStruct((T, FF), BF16), jax.ShapeDtypeStruct((FF, D), BF16)),
        in_specs=[pl.BlockSpec(memory_space=pl.ANY)] * 3,
        out_specs=[pl.BlockSpec(memory_space=pltpu.VMEM)] * 2,
        scratch_shapes=[
            vmem(4, 4, 2, T, FF),
            vmem(4, 4, 2, T, D),
            vmem(4, 4, T, D),
            vmem(FF, 2 * D),
            vmem(4, 4, T, FF),
            vmem(4, T // 2, FF), vmem(4, T // 2, FF),
            vmem(4, T, FF), vmem(4, T, FF),
            vmem(4, T, FF),
            vmem(T // 2, FF), vmem(T // 2, FF),
            vmem(T, FF), vmem(T, FF),
            vmem(FF, D, dtype=F32),
            pltpu.SemaphoreType.DMA((SENDS,)),
            pltpu.SemaphoreType.DMA((SENDS,)),
            pltpu.SemaphoreType.DMA((3,)),
            pltpu.SemaphoreType.REGULAR,
            pltpu.SemaphoreType.REGULAR,
        ],
        compiler_params=pltpu.CompilerParams(
            collective_id=0, has_side_effects=True, vmem_limit_bytes=48 << 20
        ),
        cost_estimate=pl.CostEstimate(flops=2416 << 20, bytes_accessed=4 << 20, transcendentals=0),
    )(*(pltpu.with_memory_space_constraint(v, pltpu.HBM) for v in (hidden, weight, out_grad.reshape(2, T, D))))


def solution(mesh):
    in_specs = (P("col", "row"), P("row", "col"), P("row", "col"))
    out_specs = (P("col", "row"), P("row", "col"))
    return jax.shard_map(shards, mesh=mesh, in_specs=in_specs, out_specs=out_specs, check_vma=False)
```

```python
import jax
import jax.numpy as jnp
from jax import lax
from jax.experimental import pallas as pl
from jax.experimental.pallas import tpu as pltpu
from jax.sharding import PartitionSpec as P

BF16, F32 = jnp.bfloat16, jnp.float32
FF, D, T = 1536, 384, 32
A, B = pl.ds(0, T // 2), pl.ds(T // 2, T // 2)
UNITS, GROUP, SINGLES, RECEIVERS = 75, 15, 9, 48
ORDER = [('w',), ('gz',), ('gy0',), ('hx', 0, 'b'), ('gy', 3), ('hz1',), ('hx', 0, 'a'), ('gy', 2), ('gy', 1), ('gs', 0), ('hxf', 0, 'a'), ('hxf', 0, 'b'), ('p', 0), ('rxa', 0), ('rxb', 0), ('gs', 1), ('gs', 3), ('hzfb',), ('hzfa',), ('hx', 2, 'b'), ('gs', 2), ('rf', 0), ('hz2',), ('p', 1), ('rxa', 1), ('p', 2), ('rxb', 1), ('rxa', 2), ('re', 0), ('rf', 1), ('p', 3), ('rxa', 3), ('rxb', 3), ('hs', 0), ('re', 1), ('rxb', 2), ('rf', 2), ('rz', '1'), ('wg', 0), ('rf', 3), ('hx', 2, 'a'), ('hx', 3, 'a'), ('re', 2), ('rz', '2b'), ('hx', 1, 'a'), ('hx', 1, 'b'), ('hx', 3, 'b'), ('hxf', 2, 'b'), ('hxf', 2, 'a'), ('re', 3), ('rz', '2a'), ('rz', '2c'), ('rz', '2d'), ('hxf', 1, 'a'), ('hxf', 1, 'b'), ('hxf', 3, 'a'), ('hxf', 3, 'b'), ('hs', 2), ('hs', 1), ('wg', 2), ('hs', 3), ('wg', 1), ('wg', 3)]


def kernel(
    h_ref, w_ref, g_ref, ig_ref, wg_ref,
    hall, gall, gsib, wall, part, ra, rb, r2p, r2m, summed, za, zb, z2p, z2m, acc,
    units, send_sem, single_sem, recv_sem, local_sem, near_sem, far_sem,
):
    r, c = lax.axis_index("row"), lax.axis_index("col")
    zl, y = r // 4, r % 4
    x, zh, k = c // 8, (c // 2) % 4, c % 2

    def at(dzl=0, dy=0, dx=0, dzh=0, dk=0):
        row = ((zl + dzl) % 4) * 4 + (y + dy) % 4
        col = (((x + dx) % 4) * 4 + (zh + dzh) % 4) * 2 + (k + dk) % 2
        return (row, col)

    sent, singles, receivers = [], [], {}

    def transfer(src, dst, to, wait=None):
        if wait is None:
            wait = len(receivers)
        recv = recv_sem.at[receivers.setdefault(wait, len(receivers))]
        unit = src.shape[-1] * src.shape[-2] * (src.shape[0] if len(src.shape) > 2 else 1) == T // 2 * FF
        if unit:
            sem = send_sem.at[len(sent) // GROUP]
        else:
            sem = single_sem.at[len(singles)]
        copy = pltpu.make_async_remote_copy(
            src_ref=src, dst_ref=dst, send_sem=sem, recv_sem=recv, device_id=to, device_id_type=pl.DeviceIdType.MESH
        )
        (sent if unit else singles).append(copy)
        return copy

    def send(src, dst, to, wait=None):
        copy = transfer(src, dst, to, wait)
        copy.start()
        return copy

    def wait_units(semaphore, n):
        pltpu.make_async_copy(units.at[pl.ds(0, n)], units.at[pl.ds(0, n)], semaphore).wait()

    def wait_all(wait, n=4):
        wait_units(recv_sem.at[receivers[wait]], n)

    load_w = pltpu.make_async_copy(w_ref, wall.at[:, pl.ds(0, D)], local_sem.at[0])
    load_g = pltpu.make_async_copy(g_ref, gall.at[y, zl], local_sem.at[1])
    load_h = pltpu.make_async_copy(h_ref, hall.at[zh, x, k], local_sem.at[2])
    for load in (load_g, load_h, load_w):
        load.start()

    barrier = pltpu.get_barrier_semaphore()

    def signal(semaphore, to):
        pl.semaphore_signal(semaphore, inc=1, device_id=to, device_id_type=pl.DeviceIdType.MESH)

    near = [dict(dzl=1), dict(dzl=2), dict(dzl=3), dict(dy=1), dict(dy=2), dict(dy=3), dict(dx=1), dict(dx=3)]
    for chip in near:
        signal(barrier, at(dk=1 - k, **chip))
    for chip in (dict(dzh=1), dict(dzh=3)):
        signal(barrier, at(dk=k, **chip))

    @pl.when(k == 0)
    def _():
        signal(barrier, at(dk=1))

    @pl.when(k == 1)
    def _():
        pl.semaphore_wait(barrier, 2 * len(near) + 1)
        signal(near_sem, at(dk=1))

    @pl.when(k == 0)
    def _():
        pl.semaphore_wait(near_sem, 1)

    right, left, up, down, sib = at(dx=1), at(dx=3), at(dzh=1), at(dzh=3), at(dk=1)
    xr, xl, x2 = (x + 1) % 4, (x + 3) % 4, (x + 2) % 4
    zu, zd, z2 = (zh + 1) % 4, (zh + 3) % 4, (zh + 2) % 4

    g_zl, held = {}, {}
    hx, rs, g_sib, hz, rz = {}, {}, {}, {}, {}
    load_h.wait()

    far = [z2, zd, zu, zh]
    at_y = jnp.where(y == z2, 0, jnp.where(y == zd, 1, jnp.where(y == zu, 2, 3)))
    bs = [y] + [jnp.where(i < at_y, far[i], far[i + 1]) for i in range(3)]
    zq = [zh, zd, zu, z2]

    def g_first():
        for d in (1, 3, 2):
            g_zl[d] = send(g_ref, gall.at[y, zl], at(dzl=d))

    def g_first_y():
        for d in (1, 3, 2):
            send(g_ref, gall.at[y, zl], at(dy=d), f"gy{d}")

    def w_to_sib():
        held["w"] = send(w_ref, wall.at[:, pl.ds(D, D)], sib)

    def g_along_y(d):
        g_zl[d].wait_recv()
        block = gall.at[y, (zl - d + 4) % 4]
        for dy in (1, 3, 2):
            send(block, block, at(dy=dy), f"gy{dy}")

    def g_to_sib(d):
        if d == 0:
            load_g.wait()
        else:
            wait_all(f"gy{d}")
        b = (y - d + 4) % 4
        g_sib[d] = send(gall.at[b, :, 1 - k], gsib.at[b], sib)

    def h_z_first():
        @pl.when(k == 0)
        def _():
            pl.semaphore_wait(barrier, 4)
            signal(far_sem, at(dk=1))

        @pl.when(k == 1)
        def _():
            pl.semaphore_wait(far_sem, 1)

        hz["1u"] = send(h_ref.at[A], hall.at[zh, x, k, A], up)
        hz["1d"] = send(h_ref.at[B], hall.at[zh, x, k, B], down)

    def h_z_second():
        hz["2u"] = send(h_ref.at[B], hall.at[zh, x, k, B], up)
        hz["2d"] = send(h_ref.at[A], hall.at[zh, x, k, A], down)

    def h_z_forward_up():
        hz["1u"].wait_recv()
        hz["fa"] = send(hall.at[zd, x, k, A], hall.at[zd, x, k, A], up)

    def h_z_forward_down():
        hz["1d"].wait_recv()
        hz["fb"] = send(hall.at[zu, x, k, B], hall.at[zu, x, k, B], down)

    def h_x(q, name):
        after = {(1, "b"): "2u", (2, "a"): "2d", (3, "a"): "fa", (3, "b"): "fb"}.get((q, name))
        if after:
            hz[after].wait_recv()
        block = hall.at[zq[q], x, k, A if name == "a" else B]
        hx[q, name, "r"] = send(block, block, right, None if name == "a" else f"hx{q}")
        hx[q, name, "l"] = send(block, block, left, None if name == "b" else f"hx{q}")

    def h_x_forward(q, name):
        hx[q, name, "r" if name == "a" else "l"].wait_recv()
        block = hall.at[zq[q], xl, k, A] if name == "a" else hall.at[zq[q], xr, k, B]
        send(block, block, right if name == "a" else left, f"hx{q}")

    def h_to_sib(q):
        wait_all(f"hx{q}")
        block = hall.at[zq[q], :, k]
        hx[q, "sib"] = send(block, block, sib)

    def product(j):
        if j == 0:
            load_w.wait()
            held["w"].wait_recv()
            g_sib[0].wait_recv()
        if j == 1:
            for d in (1, 3, 2):
                g_sib[d].wait_recv()
        b = bs[j]
        grads = jnp.concatenate([gall[b, :, k].reshape(4 * T, D), gsib[b].reshape(4 * T, D)], axis=1)
        for n in range(0, FF, 512):
            cols = pl.ds(n, 512)
            block = lax.dot_general(grads, wall[cols], (((1,), (1,)), ((), ())), preferred_element_type=F32)
            part[j, :, :, cols] = block.astype(BF16).reshape(4, T, 512)

    def reduce_x_far(j):
        rs[j, "1a"] = send(part.at[j, x2, A], ra.at[j], right)
        rs[j, "1b"] = send(part.at[j, x2, B], rb.at[j], left)

    def reduce_x_near(j):
        send(part.at[j, xr, B], r2p.at[j, B], right, f"rs{j}")
        send(part.at[j, xl, A], r2m.at[j, A], left, f"rs{j}")

    def reduce_x_forward(j):
        rs[j, "1a"].wait_recv()
        part[j, xr, A] = (part[j, xr, A].astype(F32) + ra[j].astype(F32)).astype(BF16)
        send(part.at[j, xr, A], r2p.at[j, A], right, f"rs{j}")
        rs[j, "1b"].wait_recv()
        part[j, xl, B] = (part[j, xl, B].astype(F32) + rb[j].astype(F32)).astype(BF16)
        send(part.at[j, xl, B], r2m.at[j, B], left, f"rs{j}")

    def reduce_x_end(j):
        wait_all(f"rs{j}")
        summed[bs[j]] = (part[j, x].astype(F32) + r2p[j].astype(F32) + r2m[j].astype(F32)).astype(BF16)

    def reduce_z(name):
        if name == "1":
            rz["1a"] = send(summed.at[z2, A], za, up)
            rz["1b"] = send(summed.at[z2, B], zb, down)
        elif name == "2a":
            send(summed.at[zu, B], z2p.at[B], up, "rz")
        elif name == "2b":
            send(summed.at[zd, A], z2m.at[A], down, "rz")
        elif name == "2c":
            rz["1a"].wait_recv()
            summed[zu, A] = (summed[zu, A].astype(F32) + za[...].astype(F32)).astype(BF16)
            send(summed.at[zu, A], z2p.at[A], up, "rz")
        elif name == "2d":
            rz["1b"].wait_recv()
            summed[zd, B] = (summed[zd, B].astype(F32) + zb[...].astype(F32)).astype(BF16)
            send(summed.at[zd, B], z2m.at[B], down, "rz")

    def weight_grad(q):
        hx[q, "sib"].wait_recv()
        grads = gall[zq[q]].reshape(8 * T, D)
        for m in range(0, FF, 512):
            rows = pl.ds(m, 512)
            block = lax.dot_general(
                hall[zq[q], :, :, :, rows].reshape(8 * T, 512), grads, (((0,), (0,)), ((), ())),
                preferred_element_type=F32,
            )
            if q == 0:
                acc[rows] = block
            elif q < 3:
                acc[rows] += block
            else:
                wg_ref[rows] = (acc[rows] + block).astype(BF16)

    steps = {
        "gy": g_along_y, "gs": g_to_sib, "hz1": h_z_first, "hz2": h_z_second, "hzfa": h_z_forward_up, "hzfb": h_z_forward_down, "hx": h_x, "hxf": h_x_forward, "hs": h_to_sib,
        "p": product, "rxa": reduce_x_far, "rxb": reduce_x_near, "gz": g_first, "gy0": g_first_y, "w": w_to_sib, "rf": reduce_x_forward, "re": reduce_x_end, "rz": reduce_z, "wg": weight_grad,
    }
    for step, *args in ORDER:
        steps[step](*args)

    wait_all("rz")
    ig_ref[...] = (summed[zh].astype(F32) + z2p[...].astype(F32) + z2m[...].astype(F32)).astype(BF16)
    for group in range(UNITS // GROUP):
        wait_units(send_sem.at[group], GROUP)
    for copy in singles:
        copy.wait_send()


def shards(hidden, weight, out_grad):
    vmem = lambda *shape, dtype=BF16: pltpu.VMEM(shape, dtype)
    return pl.pallas_call(
        kernel,
        name="mlp_backward",
        out_shape=(jax.ShapeDtypeStruct((T, FF), BF16), jax.ShapeDtypeStruct((FF, D), BF16)),
        in_specs=[pl.BlockSpec(memory_space=pl.ANY)] * 3,
        out_specs=[pl.BlockSpec(memory_space=pltpu.VMEM)] * 2,
        scratch_shapes=[
            vmem(4, 4, 2, T, FF),
            vmem(4, 4, 2, T, D),
            vmem(4, 4, T, D),
            vmem(FF, 2 * D),
            vmem(4, 4, T, FF),
            vmem(4, T // 2, FF), vmem(4, T // 2, FF),
            vmem(4, T, FF), vmem(4, T, FF),
            vmem(4, T, FF),
            vmem(T // 2, FF), vmem(T // 2, FF),
            vmem(T, FF), vmem(T, FF),
            vmem(FF, D, dtype=F32),
            vmem(GROUP, T // 2, FF),
            pltpu.SemaphoreType.DMA((UNITS // GROUP,)),
            pltpu.SemaphoreType.DMA((SINGLES,)),
            pltpu.SemaphoreType.DMA((RECEIVERS,)),
            pltpu.SemaphoreType.DMA((3,)),
            pltpu.SemaphoreType.REGULAR,
            pltpu.SemaphoreType.REGULAR,
        ],
        compiler_params=pltpu.CompilerParams(
            collective_id=0, has_side_effects=True, vmem_limit_bytes=48 << 20
        ),
        cost_estimate=pl.CostEstimate(flops=2416 << 20, bytes_accessed=4 << 20, transcendentals=0),
    )(*(pltpu.with_memory_space_constraint(v, pltpu.HBM) for v in (hidden, weight, out_grad.reshape(2, T, D))))


def solution(mesh):
    in_specs = (P("col", "row"), P("row", "col"), P("row", "col"))
    out_specs = (P("col", "row"), P("row", "col"))
    return jax.shard_map(shards, mesh=mesh, in_specs=in_specs, out_specs=out_specs, check_vma=False)
```

```python
import jax
import jax.numpy as jnp
from jax import lax
from jax.experimental import pallas as pl
from jax.experimental.pallas import tpu as pltpu
from jax.sharding import PartitionSpec as P

BF16, F32 = jnp.bfloat16, jnp.float32
FF, D, T = 1536, 384, 32
A, B = pl.ds(0, T // 2), pl.ds(T // 2, T // 2)
UNITS, GROUP, SINGLES, RECEIVERS = 75, 15, 9, 48
ORDER = [
    ("gz",), ("w",), ("gy0",), ("hx", 0, "b"), ("gy", 3), ("hz1",), ("hx", 0, "a"), ("gy", 2), ("gy", 1), ("gs", 0),
    ("hxf", 0, "a"), ("hxf", 0, "b"), ("p", 0), ("rxa", 0), ("rxb", 0), ("gs", 1), ("gs", 3), ("hzfb",), ("hzfa",),
    ("hx", 2, "b"), ("gs", 2), ("rf", 0), ("hz2",), ("p", 1), ("rxa", 1), ("p", 2), ("rxb", 1), ("rxa", 2), ("rf", 1),
    ("p", 3), ("re", 0), ("rxa", 3), ("rxb", 3), ("hs", 0), ("re", 1), ("rxb", 2), ("rf", 2), ("rz", "1"), ("wg", 0),
    ("rf", 3), ("hx", 2, "a"), ("re", 2), ("rz", "2b"), ("hx", 1, "a"), ("hx", 1, "b"), ("hx", 3, "b"), ("hxf", 2,
    "b"), ("hx", 3, "a"), ("hxf", 2, "a"), ("re", 3), ("rz", "2a"), ("rz", "2d"), ("rz", "2c"), ("hxf", 1, "a"),
    ("hxf", 1, "b"), ("hxf", 3, "b"), ("hxf", 3, "a"), ("hs", 2), ("hs", 1), ("wg", 2), ("hs", 3), ("wg", 1), ("wg",
    3),
]


def kernel(
    h_ref, w_ref, g_ref, ig_ref, wg_ref,
    hall, gall, gsib, wall, part, ra, rb, r2p, r2m, summed, za, zb, z2p, z2m, acc,
    units, send_sem, single_sem, recv_sem, local_sem, near_sem, far_sem,
):
    r, c = lax.axis_index("row"), lax.axis_index("col")
    zl, y = r // 4, r % 4
    x, zh, k = c // 8, (c // 2) % 4, c % 2

    def at(dzl=0, dy=0, dx=0, dzh=0, dk=0):
        row = ((zl + dzl) % 4) * 4 + (y + dy) % 4
        col = (((x + dx) % 4) * 4 + (zh + dzh) % 4) * 2 + (k + dk) % 2
        return (row, col)

    sent, singles, receivers = [], [], {}

    def transfer(src, dst, to, wait=None):
        if wait is None:
            wait = len(receivers)
        recv = recv_sem.at[receivers.setdefault(wait, len(receivers))]
        unit = src.shape[-1] * src.shape[-2] * (src.shape[0] if len(src.shape) > 2 else 1) == T // 2 * FF
        if unit:
            sem = send_sem.at[len(sent) // GROUP]
        else:
            sem = single_sem.at[len(singles)]
        copy = pltpu.make_async_remote_copy(
            src_ref=src, dst_ref=dst, send_sem=sem, recv_sem=recv, device_id=to, device_id_type=pl.DeviceIdType.MESH
        )
        (sent if unit else singles).append(copy)
        return copy

    def send(src, dst, to, wait=None):
        copy = transfer(src, dst, to, wait)
        copy.start()
        return copy

    def wait_units(semaphore, n):
        pltpu.make_async_copy(units.at[pl.ds(0, n)], units.at[pl.ds(0, n)], semaphore).wait()

    def wait_all(wait, n=4):
        wait_units(recv_sem.at[receivers[wait]], n)

    load_w = pltpu.make_async_copy(w_ref, wall.at[:, pl.ds(0, D)], local_sem.at[0])
    load_g = pltpu.make_async_copy(g_ref, gall.at[y, zl], local_sem.at[1])
    load_h = pltpu.make_async_copy(h_ref, hall.at[zh, x, k], local_sem.at[2])
    for load in (load_g, load_h, load_w):
        load.start()

    barrier = pltpu.get_barrier_semaphore()

    def signal(semaphore, to):
        pl.semaphore_signal(semaphore, inc=1, device_id=to, device_id_type=pl.DeviceIdType.MESH)

    near = [dict(dzl=1), dict(dzl=2), dict(dzl=3), dict(dy=1), dict(dy=2), dict(dy=3), dict(dx=1), dict(dx=3)]
    for chip in near:
        signal(barrier, at(dk=1 - k, **chip))
    for chip in (dict(dzh=1), dict(dzh=3)):
        signal(barrier, at(dk=k, **chip))

    @pl.when(k == 0)
    def _():
        signal(barrier, at(dk=1))

    @pl.when(k == 1)
    def _():
        pl.semaphore_wait(barrier, 2 * len(near) + 1)
        signal(near_sem, at(dk=1))

    @pl.when(k == 0)
    def _():
        pl.semaphore_wait(near_sem, 1)

    right, left, up, down, sib = at(dx=1), at(dx=3), at(dzh=1), at(dzh=3), at(dk=1)
    xr, xl, x2 = (x + 1) % 4, (x + 3) % 4, (x + 2) % 4
    zu, zd, z2 = (zh + 1) % 4, (zh + 3) % 4, (zh + 2) % 4

    g_zl, held = {}, {}
    hx, rs, g_sib, hz, rz = {}, {}, {}, {}, {}
    load_h.wait()

    far = [z2, zd, zu, zh]
    at_y = jnp.where(y == z2, 0, jnp.where(y == zd, 1, jnp.where(y == zu, 2, 3)))
    bs = [y] + [jnp.where(i < at_y, far[i], far[i + 1]) for i in range(3)]
    zq = [zh, zd, zu, z2]

    def g_first():
        for d in (1, 3, 2):
            g_zl[d] = send(g_ref, gall.at[y, zl], at(dzl=d))

    def g_first_y():
        for d in (1, 3, 2):
            send(g_ref, gall.at[y, zl], at(dy=d), f"gy{d}")

    def w_to_sib():
        held["w"] = send(w_ref, wall.at[:, pl.ds(D, D)], sib)

    def g_along_y(d):
        g_zl[d].wait_recv()
        block = gall.at[y, (zl - d + 4) % 4]
        for dy in (1, 3, 2):
            send(block, block, at(dy=dy), f"gy{dy}")

    def g_to_sib(d):
        if d == 0:
            load_g.wait()
        else:
            wait_all(f"gy{d}")
        b = (y - d + 4) % 4
        g_sib[d] = send(gall.at[b, :, 1 - k], gsib.at[b], sib)

    def h_z_first():
        @pl.when(k == 0)
        def _():
            pl.semaphore_wait(barrier, 4)
            signal(far_sem, at(dk=1))

        @pl.when(k == 1)
        def _():
            pl.semaphore_wait(far_sem, 1)

        hz["1u"] = send(h_ref.at[A], hall.at[zh, x, k, A], up)
        hz["1d"] = send(h_ref.at[B], hall.at[zh, x, k, B], down)

    def h_z_second():
        hz["2u"] = send(h_ref.at[B], hall.at[zh, x, k, B], up)
        hz["2d"] = send(h_ref.at[A], hall.at[zh, x, k, A], down)

    def h_z_forward_up():
        hz["1u"].wait_recv()
        hz["fa"] = send(hall.at[zd, x, k, A], hall.at[zd, x, k, A], up)

    def h_z_forward_down():
        hz["1d"].wait_recv()
        hz["fb"] = send(hall.at[zu, x, k, B], hall.at[zu, x, k, B], down)

    def h_x(q, name):
        after = {(1, "b"): "2u", (2, "a"): "2d", (3, "a"): "fa", (3, "b"): "fb"}.get((q, name))
        if after:
            hz[after].wait_recv()
        block = hall.at[zq[q], x, k, A if name == "a" else B]
        hx[q, name, "r"] = send(block, block, right, None if name == "a" else f"hx{q}")
        hx[q, name, "l"] = send(block, block, left, None if name == "b" else f"hx{q}")

    def h_x_forward(q, name):
        hx[q, name, "r" if name == "a" else "l"].wait_recv()
        block = hall.at[zq[q], xl, k, A] if name == "a" else hall.at[zq[q], xr, k, B]
        send(block, block, right if name == "a" else left, f"hx{q}")

    def h_to_sib(q):
        wait_all(f"hx{q}")
        block = hall.at[zq[q], :, k]
        hx[q, "sib"] = send(block, block, sib)

    def product(j):
        if j == 0:
            load_w.wait()
            held["w"].wait_recv()
            g_sib[0].wait_recv()
        if j == 1:
            for d in (1, 3, 2):
                g_sib[d].wait_recv()
        b = bs[j]
        grads = jnp.concatenate([gall[b, :, k].reshape(4 * T, D), gsib[b].reshape(4 * T, D)], axis=1)
        for n in range(0, FF, 512):
            cols = pl.ds(n, 512)
            block = lax.dot_general(grads, wall[cols], (((1,), (1,)), ((), ())), preferred_element_type=F32)
            part[j, :, :, cols] = block.astype(BF16).reshape(4, T, 512)

    def reduce_x_far(j):
        rs[j, "1a"] = send(part.at[j, x2, A], ra.at[j], right)
        rs[j, "1b"] = send(part.at[j, x2, B], rb.at[j], left)

    def reduce_x_near(j):
        send(part.at[j, xr, B], r2p.at[j, B], right, f"rs{j}")
        send(part.at[j, xl, A], r2m.at[j, A], left, f"rs{j}")

    def reduce_x_forward(j):
        rs[j, "1a"].wait_recv()
        part[j, xr, A] = (part[j, xr, A].astype(F32) + ra[j].astype(F32)).astype(BF16)
        send(part.at[j, xr, A], r2p.at[j, A], right, f"rs{j}")
        rs[j, "1b"].wait_recv()
        part[j, xl, B] = (part[j, xl, B].astype(F32) + rb[j].astype(F32)).astype(BF16)
        send(part.at[j, xl, B], r2m.at[j, B], left, f"rs{j}")

    def reduce_x_end(j):
        wait_all(f"rs{j}")
        summed[bs[j]] = (part[j, x].astype(F32) + r2p[j].astype(F32) + r2m[j].astype(F32)).astype(BF16)

    def reduce_z(name):
        if name == "1":
            rz["1a"] = send(summed.at[z2, A], za, up)
            rz["1b"] = send(summed.at[z2, B], zb, down)
        elif name == "2a":
            send(summed.at[zu, B], z2p.at[B], up, "rz")
        elif name == "2b":
            send(summed.at[zd, A], z2m.at[A], down, "rz")
        elif name == "2c":
            rz["1a"].wait_recv()
            summed[zu, A] = (summed[zu, A].astype(F32) + za[...].astype(F32)).astype(BF16)
            send(summed.at[zu, A], z2p.at[A], up, "rz")
        elif name == "2d":
            rz["1b"].wait_recv()
            summed[zd, B] = (summed[zd, B].astype(F32) + zb[...].astype(F32)).astype(BF16)
            send(summed.at[zd, B], z2m.at[B], down, "rz")

    def weight_grad(q):
        hx[q, "sib"].wait_recv()
        grads = gall[zq[q]].reshape(8 * T, D)
        for m in range(0, FF, 512):
            rows = pl.ds(m, 512)
            block = lax.dot_general(
                hall[zq[q], :, :, :, rows].reshape(8 * T, 512), grads, (((0,), (0,)), ((), ())),
                preferred_element_type=F32,
            )
            if q == 0:
                acc[rows] = block
            elif q < 3:
                acc[rows] += block
            else:
                wg_ref[rows] = (acc[rows] + block).astype(BF16)

    steps = {
        "gy": g_along_y, "gs": g_to_sib, "hz1": h_z_first, "hz2": h_z_second, "hzfa": h_z_forward_up, "hzfb": h_z_forward_down, "hx": h_x, "hxf": h_x_forward, "hs": h_to_sib,
        "p": product, "rxa": reduce_x_far, "rxb": reduce_x_near, "gz": g_first, "gy0": g_first_y, "w": w_to_sib, "rf": reduce_x_forward, "re": reduce_x_end, "rz": reduce_z, "wg": weight_grad,
    }
    for step, *args in ORDER:
        steps[step](*args)

    wait_all("rz")
    ig_ref[...] = (summed[zh].astype(F32) + z2p[...].astype(F32) + z2m[...].astype(F32)).astype(BF16)
    for group in range(UNITS // GROUP):
        wait_units(send_sem.at[group], GROUP)
    for copy in singles:
        copy.wait_send()


def shards(hidden, weight, out_grad):
    vmem = lambda *shape, dtype=BF16: pltpu.VMEM(shape, dtype)
    return pl.pallas_call(
        kernel,
        name="mlp_backward",
        out_shape=(jax.ShapeDtypeStruct((T, FF), BF16), jax.ShapeDtypeStruct((FF, D), BF16)),
        in_specs=[pl.BlockSpec(memory_space=pl.ANY)] * 3,
        out_specs=[pl.BlockSpec(memory_space=pltpu.VMEM)] * 2,
        scratch_shapes=[
            vmem(4, 4, 2, T, FF),
            vmem(4, 4, 2, T, D),
            vmem(4, 4, T, D),
            vmem(FF, 2 * D),
            vmem(4, 4, T, FF),
            vmem(4, T // 2, FF), vmem(4, T // 2, FF),
            vmem(4, T, FF), vmem(4, T, FF),
            vmem(4, T, FF),
            vmem(T // 2, FF), vmem(T // 2, FF),
            vmem(T, FF), vmem(T, FF),
            vmem(FF, D, dtype=F32),
            vmem(GROUP, T // 2, FF),
            pltpu.SemaphoreType.DMA((UNITS // GROUP,)),
            pltpu.SemaphoreType.DMA((SINGLES,)),
            pltpu.SemaphoreType.DMA((RECEIVERS,)),
            pltpu.SemaphoreType.DMA((3,)),
            pltpu.SemaphoreType.REGULAR,
            pltpu.SemaphoreType.REGULAR,
        ],
        compiler_params=pltpu.CompilerParams(
            collective_id=0, has_side_effects=True, vmem_limit_bytes=48 << 20
        ),
        cost_estimate=pl.CostEstimate(flops=2416 << 20, bytes_accessed=4 << 20, transcendentals=0),
    )(*(pltpu.with_memory_space_constraint(v, pltpu.HBM) for v in (hidden, weight, out_grad.reshape(2, T, D))))


def solution(mesh):
    in_specs = (P("col", "row"), P("row", "col"), P("row", "col"))
    out_specs = (P("col", "row"), P("row", "col"))
    return jax.shard_map(shards, mesh=mesh, in_specs=in_specs, out_specs=out_specs, check_vma=False)
```
